768 devices in a mesh: dp: 48 (over z_lo, y), mx: 8 (over x, z_hi), my: 2 (over core).
Axes of the slice: x: 4, y: 8, z: 12 (z_hi: 2, z_lo: 6; z = z_hi * 6 + z_lo), core: 2. Of those that a mesh axis runs over, the one named last changes fastest.
Arguments:
- normed: bfloat16 [18432, 6144], P(('dp', 'mx'), 'my'), may hold values from -24 to 24
- weight: bfloat16 [6144, 3072], P('my', 'mx'), may hold values from -0.078125 to 0.078125
- cotangent: bfloat16 [18432, 3072], P('dp', 'mx'), may hold values from -6 to 6
- head_gain: float32 [128], replicated, may hold values from 0.1 to 1.9
Outputs:
- input_grad: bfloat16 [18432, 6144], P(('dp', 'mx'), 'my')
- weight_grad: float32 [6144, 3072], P(('my', 'dp'), 'mx')
The draws below stay inside these ranges and needn't reach their ends.
All inputs are finite; a program needn't handle non-finite values.
Results may differ from the reference program's by a relative error of at most 0.0049.
Values may be sent and summed in bfloat16 or wider, within the bound.
No kernel may reach another device: no remote copies, remote signals or barrier semaphores. Data moves between devices by JAX's collectives and lax.ppermute only.
A program may use at most 64 MiB of HBM per device.

```python
import math
import jax
import jax.numpy as jnp
from jax import lax

D = 6144
HD = 128
QW = 3072
TOKENS = 18432


def spiked(entries, own_key, source, target, shards_of, factor):
    def block_of(dim):
        return (jnp.arange(entries.shape[dim]) // (entries.shape[dim] // shards_of)).reshape((-1,) + (1,) * (entries.ndim - 1 - dim))

    near = jax.random.permutation(own_key, shards_of)[block_of(target)]
    far = (block_of(target) + shards_of // 2) % shards_of
    return jnp.where((block_of(source) == near) | (block_of(source) == far), factor * entries, entries)


def block_levels(own_key, dims, pieces, least, largest):
    def one(position, parts):
        heights = jax.random.uniform(jax.random.fold_in(jax.random.fold_in(own_key, 6), position), (parts,), jnp.float32, least / len(pieces), largest / len(pieces))
        return jnp.repeat(jnp.exp(heights), dims[position] // parts).reshape((-1,) + (1,) * (len(dims) - position - 1))

    level = one(*pieces[0])
    for cut in pieces[1:]:
        level = level * one(*cut)
    return level


def gaussian(rng, extent, deviation, reach, split=(), kind=jnp.bfloat16):
    values = deviation * jax.random.normal(rng, extent, jnp.float32)
    if split:
        values = values * block_levels(rng, extent, split, -0.22, 0.18)
    return jnp.clip(values, -reach, reach).astype(kind)


def bell_draw_with(own_key, extent, spread, reach, split, heavy, held_as=jnp.bfloat16):
    values = spread * jax.random.normal(own_key, extent, jnp.float32)
    if split:
        values = values * block_levels(own_key, extent, split, -0.22, 0.18)
    return jnp.clip(spiked(values, jax.random.fold_in(own_key, 3), *heavy), -reach, reach).astype(held_as)


def setup_inputs(seed: int = 0) -> dict:
    seeds = jax.random.split(jax.random.key(seed), 5)
    return {
        "normed": bell_draw_with(seeds[0], (TOKENS, D), 1.0, 24.0, ((0, 384), (1, 2)), (0, 1, 384, 6.0)),
        "weight": gaussian(seeds[1], (D, QW), D ** -0.5, 0.078125, ((0, 2), (1, 8))),
        "cotangent": gaussian(seeds[2], (TOKENS, QW), 1.0, 6.0, ((0, 48), (1, 8))),
        "head_gain": jnp.clip(1.0 + 0.18 * jax.random.normal(seeds[3], (HD,), jnp.float32), 0.1, 1.9),
    }


def head_backward(pre, cot, gain):
    rows = pre.shape[0]
    pre3 = pre.reshape(rows, -1, gain.shape[0])
    centred = pre3 - lax.optimization_barrier(jnp.mean(pre3, axis=-1, keepdims=True))
    inverse = lax.rsqrt(lax.optimization_barrier(jnp.mean(centred * centred, axis=-1, keepdims=True)) + 1e-06)
    unit = centred * inverse
    scaled = cot.astype(jnp.float32).reshape(pre3.shape) * gain
    result = inverse * (scaled - lax.optimization_barrier(jnp.mean(scaled, axis=-1, keepdims=True)) - unit * lax.optimization_barrier(jnp.mean(scaled * unit, axis=-1, keepdims=True)))
    return result.reshape(rows, -1).astype(jnp.bfloat16)

def reference(normed, weight, cotangent, head_gain):
    wide_in = normed.astype(jnp.float32)
    wide_w = weight.astype(jnp.float32)
    pre = jnp.dot(wide_in, wide_w, precision=lax.Precision.HIGHEST)
    head_rows = head_backward(pre, cotangent, head_gain)
    wide_rows = head_rows.astype(jnp.float32)
    weight_grad = jnp.dot(wide_in.T, wide_rows, precision=lax.Precision.HIGHEST) * (1.0 / math.sqrt(TOKENS))
    input_grad = jnp.dot(wide_rows, wide_w.T, precision=lax.Precision.HIGHEST).astype(jnp.bfloat16)
    return (input_grad, weight_grad)
```

```python
import math

import jax
import jax.numpy as jnp
from jax import lax
from jax.sharding import Mesh, PartitionSpec as P

F32 = jnp.float32
BF16 = jnp.bfloat16


def head_backward(pre, cot, gain):
    rows = pre.shape[0]
    pre3 = pre.reshape(rows, -1, gain.shape[0])
    centred = pre3 - jnp.mean(pre3, axis=-1, keepdims=True)
    inverse = lax.rsqrt(jnp.mean(centred * centred, axis=-1, keepdims=True) + 1e-06)
    unit = centred * inverse
    scaled = cot.astype(F32).reshape(pre3.shape) * gain
    result = inverse * (
        scaled
        - jnp.mean(scaled, axis=-1, keepdims=True)
        - unit * jnp.mean(scaled * unit, axis=-1, keepdims=True)
    )
    return result.reshape(rows, -1).astype(BF16)


def shift(value, axis, by):
    size = lax.axis_size(axis)
    return lax.ppermute(value, axis, [(i, (i + by) % size) for i in range(size)])


def body(normed, weight, cotangent, head_gain):
    nx, ny, nz, nh = (lax.axis_size(a) for a in ("x", "y", "zl", "zh"))
    rows, width = normed.shape
    heads = weight.shape[1]
    x, y, zl, zh = (lax.axis_index(a) for a in ("x", "y", "zl", "zh"))

    peer = shift(normed, "zh", 1)
    own = [normed] + [shift(normed, "x", k) for k in range(1, nx)]
    other = [peer] + [shift(peer, "x", k) for k in range(1, nx)]
    gathered = jnp.concatenate([p for pair in zip(own, other) for p in pair], axis=0)

    cot = cotangent.reshape(nx, nh, rows, heads)
    order_x = (x - jnp.arange(nx)) % nx
    order_h = (zh + jnp.arange(nh)) % nh
    cot = cot[order_x][:, order_h].reshape(nx * nh * rows, heads)

    partial_value = jnp.dot(gathered, weight, preferred_element_type=F32)
    summed = partial_value + shift(partial_value, "c", 1)
    head_rows = head_backward(summed, cot, head_gain)

    factor = 1.0 / math.sqrt(rows * nx * nh * ny * nz)
    term = lax.dot_general(
        gathered, head_rows, (((0,), (0,)), ((), ())), preferred_element_type=F32
    )
    term = (term * factor).astype(BF16).reshape(nz, ny, -1, heads).swapaxes(0, 1)
    over_y = lax.psum_scatter(term, "y", scatter_dimension=0, tiled=True)[0]

    back = lax.dot_general(
        head_rows, weight, (((1,), (1,)), ((), ())), preferred_element_type=F32
    ).astype(BF16).reshape(nx, nh, rows, width)
    total = back[0].astype(F32)
    for k in range(1, nx):
        total = total + shift(back[k], "x", -k).astype(F32)
    input_grad = (total[0] + shift(total[1].astype(BF16), "zh", 1).astype(F32)).astype(BF16)

    weight_grad = lax.dynamic_index_in_dim(over_y, zl, 0, False).astype(F32)
    for k in range(1, nz):
        chunk = lax.dynamic_index_in_dim(over_y, (zl + k) % nz, 0, False)
        weight_grad = weight_grad + shift(chunk, "zl", k).astype(F32)
    return (input_grad, weight_grad)


def spread(fine):
    return jax.shard_map(
        body,
        mesh=fine,
        in_specs=(
            P(("zl", "y", "x", "zh"), "c"),
            P("c", ("x", "zh")),
            P(("zl", "y"), ("x", "zh")),
            P(),
        ),
        out_specs=(P(("zl", "y", "x", "zh"), "c"), P(("c", "zl", "y"), ("x", "zh"))),
        check_vma=False,
    )


def solution(mesh):
    return spread(Mesh(mesh.devices.reshape(6, 8, 4, 2, 2), ("zl", "y", "x", "zh", "c")))
```

```python
import functools
import math

import jax
import jax.numpy as jnp
from jax import lax
from jax.experimental import pallas as pl
from jax.experimental.pallas import tpu as pltpu
from jax.sharding import Mesh, PartitionSpec as P

F32 = jnp.float32
BF16 = jnp.bfloat16


def mean(value):
    return jnp.mean(value, axis=-1, keepdims=True)


def rows_kernel(sizes, factor, where, mine, theirs, cot, gain, tokens, rows_out, *rest):
    nx, nh, ny, nz = sizes
    outs, term = rest[:-1], rest[-1]
    x, zh, y = where[0], where[1], where[2]
    count = tokens.shape[0] // (nx * nh)
    heads = mine.shape[1]
    hd = gain.shape[1]
    for kx in range(nx):
        for kh in range(nh):
            block = lax.rem(x - kx + nx, nx) * nh + lax.rem(zh + kh, nh)
            span = pl.ds((kx * nh + kh) * count, count)
            for h in range(0, heads, hd):
                pre = mine[span, h : h + hd] + theirs[span, h : h + hd]
                centred = pre - mean(pre)
                inverse = lax.rsqrt(mean(centred * centred) + 1e-06)
                unit = centred * inverse
                scaled = cot[block, :, h : h + hd].astype(F32) * gain[...]
                result = inverse * (scaled - mean(scaled) - unit * mean(scaled * unit))
                rows_out[span, h : h + hd] = result.astype(BF16)
    rows = rows_out[...]
    part = tokens.shape[1] // nz
    blk = part // ny
    for z in range(nz):
        term[...] = factor * lax.dot_general(
            tokens[:, z * part : (z + 1) * part],
            rows,
            (((0,), (0,)), ((), ())),
            preferred_element_type=F32,
        )
        for k in range(ny):
            at = pl.multiple_of(lax.rem(y + k, ny) * blk, blk)
            outs[k][z] = term[pl.ds(at, blk), :].astype(BF16)


def rows_and_chunks(sizes, factor, where, mine, theirs, cot, gain, tokens):
    nx, nh, ny, nz = sizes
    heads = mine.shape[1]
    part = tokens.shape[1] // nz
    vmem = pl.BlockSpec(memory_space=pltpu.VMEM)
    chunk = jax.ShapeDtypeStruct((nz, part // ny, heads), BF16)
    return pl.pallas_call(
        functools.partial(rows_kernel, sizes, factor),
        out_shape=[jax.ShapeDtypeStruct(mine.shape, BF16)] + [chunk] * ny,
        in_specs=[pl.BlockSpec(memory_space=pltpu.SMEM)] + [vmem] * 5,
        out_specs=[vmem] * (ny + 1),
        scratch_shapes=[pltpu.VMEM((part, heads), F32)],
        compiler_params=pltpu.CompilerParams(vmem_limit_bytes=40 * 2**20),
        name="rows_and_chunks",
    )(where, mine, theirs, cot, gain, tokens)


def shift(value, axis, by):
    size = lax.axis_size(axis)
    return lax.ppermute(value, axis, [(i, (i + by) % size) for i in range(size)])


def add(*terms):
    total = terms[0].astype(F32)
    for t in terms[1:]:
        total = total + t.astype(F32)
    return total


def body(normed, weight, cotangent, head_gain):
    nx, ny, nz, nh = (lax.axis_size(a) for a in ("x", "y", "zl", "zh"))
    count, width = normed.shape
    heads = weight.shape[1]
    where = jnp.stack([lax.axis_index(a) for a in ("x", "zh", "y")]).astype(jnp.int32)

    peer = shift(normed, "zh", 1)
    own = [normed] + [shift(normed, "x", k) for k in range(1, nx)]
    other = [peer] + [shift(peer, "x", k) for k in range(1, nx)]
    tokens = jnp.concatenate([p for pair in zip(own, other) for p in pair], axis=0)

    mine = jnp.dot(tokens, weight, preferred_element_type=F32)
    theirs = shift(mine, "c", 1)
    factor = 1.0 / math.sqrt(count * nx * nh * ny * nz)
    rows, *c = rows_and_chunks(
        (nx, nh, ny, nz),
        factor,
        where,
        mine,
        theirs,
        cotangent.reshape(nx * nh, count, heads),
        head_gain.reshape(1, -1),
        tokens,
    )

    half = c[4].shape[1] // 2
    from3, from5 = shift(c[3], "y", 1), shift(c[5], "y", -1)
    low = shift(c[4][:, :half], "y", 2)
    high = shift(c[4][:, half:], "y", -2)
    near1, near7 = shift(c[1], "y", 1), shift(c[7], "y", -1)
    up = add(c[2], from3) + jnp.pad(low.astype(F32), ((0, 0), (0, half), (0, 0)))
    down = add(c[6], from5) + jnp.pad(high.astype(F32), ((0, 0), (half, 0), (0, 0)))
    near2, near6 = shift(up.astype(BF16), "y", 2), shift(down.astype(BF16), "y", -2)

    back = [
        lax.dot_general(
            rows[k * nh * count : (k + 1) * nh * count],
            weight,
            (((1,), (1,)), ((), ())),
            preferred_element_type=F32,
        ).astype(BF16)
        for k in range(nx)
    ]
    total = add(back[0], *[shift(back[k], "x", -k) for k in range(1, nx)])
    far = shift(total[count:].astype(BF16), "zh", 1)
    input_grad = add(total[:count], far).astype(BF16)

    over_y = add(c[0], near1, near7, near2, near6).astype(BF16)
    pieces = lax.all_to_all(over_y, "zl", 0, 0, tiled=True)
    weight_grad = jnp.sum(pieces.astype(F32), axis=0)
    return (input_grad, weight_grad)


def spread(fine):
    return jax.shard_map(
        body,
        mesh=fine,
        in_specs=(
            P(("zl", "y", "x", "zh"), "c"),
            P("c", ("x", "zh")),
            P(("zl", "y"), ("x", "zh")),
            P(),
        ),
        out_specs=(P(("zl", "y", "x", "zh"), "c"), P(("c", "zl", "y"), ("x", "zh"))),
        check_vma=False,
    )


def solution(mesh):
    return spread(Mesh(mesh.devices.reshape(6, 8, 4, 2, 2), ("zl", "y", "x", "zh", "c")))
```

```python
import functools
import math

import jax
import jax.numpy as jnp
from jax import lax
from jax.experimental import pallas as pl
from jax.experimental.pallas import tpu as pltpu
from jax.sharding import Mesh, PartitionSpec as P

F32 = jnp.float32
BF16 = jnp.bfloat16
ORDER = ((3, 1), (5, 7), (4,), (2,), (6,), (0,))


def mean(value):
    return jnp.mean(value, axis=-1, keepdims=True)


def rows_kernel(sizes, factor, where, mine, theirs, cot, gain, tokens, rows_out, *rest):
    nx, nh, ny, nz = sizes
    outs, term = rest[:-1], rest[-1]
    x, zh, y = where[0], where[1], where[2]
    count = tokens.shape[0] // (nx * nh)
    heads = mine.shape[1]
    hd = gain.shape[1]
    for kx in range(nx):
        for kh in range(nh):
            block = lax.rem(x - kx + nx, nx) * nh + lax.rem(zh + kh, nh)
            span = pl.ds((kx * nh + kh) * count, count)
            for h in range(0, heads, hd):
                pre = mine[span, h : h + hd] + theirs[span, h : h + hd]
                centred = pre - mean(pre)
                inverse = lax.rsqrt(mean(centred * centred) + 1e-06)
                unit = centred * inverse
                scaled = cot[block, :, h : h + hd].astype(F32) * gain[...]
                result = inverse * (scaled - mean(scaled) - unit * mean(scaled * unit))
                rows_out[span, h : h + hd] = result.astype(BF16)
    rows = rows_out[...]
    part = tokens.shape[1] // nz
    blk = part // ny
    for z in range(nz):
        term[...] = factor * lax.dot_general(
            tokens[:, z * part : (z + 1) * part],
            rows,
            (((0,), (0,)), ((), ())),
            preferred_element_type=F32,
        )
        for out, ks in zip(outs, ORDER):
            for i, k in enumerate(ks):
                at = pl.multiple_of(lax.rem(y + k, ny) * blk, blk)
                out[i, z] = term[pl.ds(at, blk), :].astype(BF16)


def rows_and_chunks(sizes, factor, where, mine, theirs, cot, gain, tokens):
    nx, nh, ny, nz = sizes
    heads = mine.shape[1]
    part = tokens.shape[1] // nz
    vmem = pl.BlockSpec(memory_space=pltpu.VMEM)
    chunks = [jax.ShapeDtypeStruct((len(ks), nz, part // ny, heads), BF16) for ks in ORDER]
    return pl.pallas_call(
        functools.partial(rows_kernel, sizes, factor),
        out_shape=[jax.ShapeDtypeStruct(mine.shape, BF16)] + chunks,
        in_specs=[pl.BlockSpec(memory_space=pltpu.SMEM)] + [vmem] * 5,
        out_specs=[vmem] * (len(ORDER) + 1),
        scratch_shapes=[pltpu.VMEM((part, heads), F32)],
        compiler_params=pltpu.CompilerParams(vmem_limit_bytes=8 * 2**20),
        name="rows_and_chunks",
    )(where, mine, theirs, cot, gain, tokens)


def shift(value, axis, by):
    size = lax.axis_size(axis)
    return lax.ppermute(value, axis, [(i, (i + by) % size) for i in range(size)])


def add(*terms):
    total = terms[0].astype(F32)
    for t in terms[1:]:
        total = total + t.astype(F32)
    return total


def body(normed, weight, cotangent, head_gain):
    nx, ny, nz, nh = (lax.axis_size(a) for a in ("x", "y", "zl", "zh"))
    count, width = normed.shape
    heads = weight.shape[1]
    where = jnp.stack([lax.axis_index(a) for a in ("x", "zh", "y")]).astype(jnp.int32)

    peer = shift(normed, "zh", 1)
    own1, own3 = shift(normed, "x", 1), shift(normed, "x", -1)
    both = jnp.concatenate([normed, peer], axis=0)
    both2 = shift(both, "x", 2)
    peer1, peer3 = shift(peer, "x", 1), shift(peer, "x", -1)
    tokens = jnp.concatenate([both, own1, peer1, both2, own3, peer3], axis=0)

    mine = jnp.dot(tokens, weight, preferred_element_type=F32)
    theirs = shift(mine, "c", 1)
    factor = 1.0 / math.sqrt(count * nx * nh * ny * nz)
    rows, *c = rows_and_chunks(
        (nx, nh, ny, nz),
        factor,
        where,
        mine,
        theirs,
        cotangent.reshape(nx * nh, count, heads),
        head_gain.reshape(1, -1),
        tokens,
    )

    up, down, across, two, six, own = c
    core = lax.axis_index("c")
    turn = [
        (i * 2 + j, (i + (2, -2)[j]) % ny * 2 + j) for i in range(ny) for j in range(2)
    ]
    got_up, got_down = shift(up, "y", 1), shift(down, "y", -1)
    got4 = lax.ppermute(across[0], ("y", "c"), turn).astype(F32)
    two = add(two[0], got_up[0], jnp.where(core == 0, got4, 0.0)).astype(BF16)
    six = add(six[0], got_down[0], jnp.where(core == 1, got4, 0.0)).astype(BF16)
    got2, got6 = shift(two, "y", 2), shift(six, "y", -2)

    back = [
        lax.dot_general(
            rows[k * nh * count : (k + 1) * nh * count],
            weight,
            (((1,), (1,)), ((), ())),
            preferred_element_type=F32,
        )
        for k in range(nx)
    ]
    terms = [back[0]] + [shift(back[k].astype(BF16), "x", -k) for k in (2, 1, 3)]
    far = shift(add(*[t[count:] for t in terms]).astype(BF16), "zh", 1)
    input_grad = add(*[t[:count] for t in terms], far).astype(BF16)

    over_y = add(own[0], got_up[1], got_down[1], got2, got6)
    third = nz // 2
    zl = lax.axis_index("zl")
    over_y = over_y.reshape(2, third, -1, heads)
    place = zl % third

    def of_third(k):
        return lax.dynamic_index_in_dim(over_y, (place + k) % third, 1, False)

    kept = of_third(0)
    for k in range(1, third):
        hop = [(i, i // third * third + (i + k) % third) for i in range(nz)]
        kept = add(kept, lax.ppermute(of_third(k).astype(BF16), "zl", hop))
    side = zl // third
    last = shift(lax.dynamic_index_in_dim(kept, 1 - side, 0, False).astype(BF16), "zl", third)
    weight_grad = add(lax.dynamic_index_in_dim(kept, side, 0, False), last)
    return (input_grad, weight_grad)


def spread(fine):
    return jax.shard_map(
        body,
        mesh=fine,
        in_specs=(
            P(("zl", "y", "x", "zh"), "c"),
            P("c", ("x", "zh")),
            P(("zl", "y"), ("x", "zh")),
            P(),
        ),
        out_specs=(P(("zl", "y", "x", "zh"), "c"), P(("c", "zl", "y"), ("x", "zh"))),
        check_vma=False,
    )


def solution(mesh):
    return spread(Mesh(mesh.devices.reshape(6, 8, 4, 2, 2), ("zl", "y", "x", "zh", "c")))
```

```python
import functools
import math

import jax
import jax.numpy as jnp
from jax import lax
from jax.experimental import pallas as pl
from jax.experimental.pallas import tpu as pltpu
from jax.sharding import Mesh, PartitionSpec as P

F32 = jnp.float32
BF16 = jnp.bfloat16
ORDER = ((3, 1), (5, 7), (4,), (2,), (6,), (0,))


def mean(value):
    return jnp.mean(value, axis=-1, keepdims=True)


def rows_kernel(sizes, factor, where, mine, theirs, cot, cot_far, gain, tokens, rows_out, *rest):
    nx, nh, ny, nz = sizes
    outs, (held, term, sem) = rest[:-3], rest[-3:]
    x, y = where[0], where[1]
    copy = pltpu.make_async_copy(tokens, held, sem)
    copy.start()
    count = cot.shape[1]
    heads = mine.shape[1]
    hd = gain.shape[1]
    for kx in range(nx):
        block = lax.rem(x - kx + nx, nx)
        for kh in range(nh):
            span = pl.ds((kx * nh + kh) * count, count)
            side = (cot, cot_far)[kh]
            for h in range(0, heads, hd):
                pre = mine[span, h : h + hd] + theirs[span, h : h + hd]
                centred = pre - mean(pre)
                inverse = lax.rsqrt(mean(centred * centred) + 1e-06)
                unit = centred * inverse
                scaled = side[block, :, h : h + hd].astype(F32) * gain[...]
                result = inverse * (scaled - mean(scaled) - unit * mean(scaled * unit))
                rows_out[span, h : h + hd] = result.astype(BF16)
    rows = rows_out[...]
    part = held.shape[1] // nz
    blk = part // ny
    copy.wait()
    for z in range(nz):
        term[...] = factor * lax.dot_general(
            held[:, z * part : (z + 1) * part],
            rows,
            (((0,), (0,)), ((), ())),
            preferred_element_type=F32,
        )
        for out, ks in zip(outs, ORDER):
            for i, k in enumerate(ks):
                at = pl.multiple_of(lax.rem(y + k, ny) * blk, blk)
                out[i, z] = term[pl.ds(at, blk), :].astype(BF16)


def rows_and_chunks(sizes, factor, where, mine, theirs, cot, cot_far, gain, tokens):
    nx, nh, ny, nz = sizes
    heads = mine.shape[1]
    part = tokens.shape[1] // nz
    vmem = pl.BlockSpec(memory_space=pltpu.VMEM)
    chunks = [jax.ShapeDtypeStruct((len(ks), nz, part // ny, heads), BF16) for ks in ORDER]
    return pl.pallas_call(
        functools.partial(rows_kernel, sizes, factor),
        out_shape=[jax.ShapeDtypeStruct(mine.shape, BF16)] + chunks,
        in_specs=[pl.BlockSpec(memory_space=pltpu.SMEM)]
        + [vmem] * 5
        + [pl.BlockSpec(memory_space=pl.ANY)],
        out_specs=[vmem] * (len(ORDER) + 1),
        scratch_shapes=[
            pltpu.VMEM(tokens.shape, BF16),
            pltpu.VMEM((part, heads), F32),
            pltpu.SemaphoreType.DMA,
        ],
        compiler_params=pltpu.CompilerParams(vmem_limit_bytes=12 * 2**20),
        name="rows_and_chunks",
    )(where, mine, theirs, cot, cot_far, gain, tokens)


def shift(value, axis, by):
    size = lax.axis_size(axis)
    return lax.ppermute(value, axis, [(i, (i + by) % size) for i in range(size)])


def add(*terms):
    total = terms[0].astype(F32)
    for t in terms[1:]:
        total = total + t.astype(F32)
    return total


def body(normed, weight, cotangent, head_gain):
    nx, ny, nz, nh = (lax.axis_size(a) for a in ("x", "y", "zl", "zh"))
    count, width = normed.shape
    heads = weight.shape[1]
    where = jnp.stack([lax.axis_index(a) for a in ("x", "y")]).astype(jnp.int32)
    zh = lax.axis_index("zh")

    def mirror(value):
        ends = [(i, nz * nh - 1 - i) for i in range(nz * nh)]
        return lax.ppermute(value, ("zl", "zh"), ends)

    peer = mirror(normed)
    own = [normed] + [shift(normed, "x", k) for k in (1, 2, 3)]
    cot = cotangent.reshape(nx, nh, count, heads)
    cot_far = lax.dynamic_index_in_dim(cot, 1 - zh, 1, False)
    cot_far = lax.ppermute(cot_far, "zl", [(i, nz - 1 - i) for i in range(nz)])
    cot = lax.dynamic_index_in_dim(cot, zh, 1, False)
    other = [peer] + [shift(peer, "x", k) for k in (1, 2, 3)]
    tokens = jnp.concatenate([p for pair in zip(own, other) for p in pair], axis=0)

    mine = jnp.dot(tokens, weight, preferred_element_type=F32)
    theirs = shift(mine, "c", 1)
    factor = 1.0 / math.sqrt(count * nx * nh * ny * nz)
    rows, *c = rows_and_chunks(
        (nx, nh, ny, nz),
        factor,
        where,
        mine,
        theirs,
        cot,
        cot_far,
        head_gain.reshape(1, -1),
        tokens,
    )

    up, down, across, two, six, own = c
    core = lax.axis_index("c")
    turn = [
        (i * 2 + j, (i + (2, -2)[j]) % ny * 2 + j) for i in range(ny) for j in range(2)
    ]
    got_up, got_down = shift(up, "y", 1), shift(down, "y", -1)
    got4 = lax.ppermute(across[0], ("y", "c"), turn).astype(F32)
    two = add(two[0], got_up[0], jnp.where(core == 0, got4, 0.0)).astype(BF16)
    six = add(six[0], got_down[0], jnp.where(core == 1, got4, 0.0)).astype(BF16)
    got2, got6 = shift(two, "y", 2), shift(six, "y", -2)

    back = [
        lax.dot_general(
            rows[k * nh * count : (k + 1) * nh * count],
            weight,
            (((1,), (1,)), ((), ())),
            preferred_element_type=F32,
        )
        for k in range(nx)
    ]
    terms = [back[0]] + [shift(back[k].astype(BF16), "x", -k) for k in (2, 1, 3)]
    far = mirror(add(*[t[count:] for t in terms]).astype(BF16))
    input_grad = add(*[t[:count] for t in terms], far).astype(BF16)

    over_y = add(own[0], got_up[1], got_down[1], got2, got6)
    third = nz // 2
    zl = lax.axis_index("zl")
    over_y = over_y.reshape(2, third, -1, heads)
    place = zl % third

    def of_third(k):
        return lax.dynamic_index_in_dim(over_y, (place + k) % third, 1, False)

    kept = of_third(0)
    for k in range(1, third):
        hop = [(i, i // third * third + (i + k) % third) for i in range(nz)]
        kept = add(kept, lax.ppermute(of_third(k).astype(BF16), "zl", hop))
    side = zl // third
    last = shift(lax.dynamic_index_in_dim(kept, 1 - side, 0, False).astype(BF16), "zl", third)
    weight_grad = add(lax.dynamic_index_in_dim(kept, side, 0, False), last)
    return (input_grad, weight_grad)


def spread(fine):
    return jax.shard_map(
        body,
        mesh=fine,
        in_specs=(
            P(("zl", "y", "x", "zh"), "c"),
            P("c", ("x", "zh")),
            P(("zl", "y"), ("x", "zh")),
            P(),
        ),
        out_specs=(P(("zl", "y", "x", "zh"), "c"), P(("c", "zl", "y"), ("x", "zh"))),
        check_vma=False,
    )


def solution(mesh):
    return spread(Mesh(mesh.devices.reshape(6, 8, 4, 2, 2), ("zl", "y", "x", "zh", "c")))
```

```python
import functools
import math

import jax
import jax.numpy as jnp
from jax import lax
from jax.experimental import pallas as pl
from jax.experimental.pallas import tpu as pltpu
from jax.sharding import Mesh, PartitionSpec as P

F32 = jnp.float32
BF16 = jnp.bfloat16
ORDER = ((3, 1), (5, 7), (4,), (2,), (6,), (0,))


def mean(value):
    return jnp.mean(value, axis=-1, keepdims=True)


def rows_kernel(sizes, factor, where, mine, theirs, cot, cot_far, gain, tokens, rows_out, *rest):
    nx, nh, ny, nz = sizes
    outs, term = rest[:-1], rest[-1]
    x, y = where[0], where[1]
    count = cot.shape[1]
    heads = mine.shape[1]
    hd = gain.shape[1]
    for kx in range(nx):
        block = lax.rem(x - kx + nx, nx)
        for kh in range(nh):
            span = pl.ds((kx * nh + kh) * count, count)
            side = (cot, cot_far)[kh]
            for h in range(0, heads, hd):
                pre = mine[span, h : h + hd] + theirs[span, h : h + hd]
                centred = pre - mean(pre)
                inverse = lax.rsqrt(mean(centred * centred) + 1e-06)
                unit = centred * inverse
                scaled = side[block, :, h : h + hd].astype(F32) * gain[...]
                result = inverse * (scaled - mean(scaled) - unit * mean(scaled * unit))
                rows_out[span, h : h + hd] = result.astype(BF16)
    rows = rows_out[...]
    part = tokens.shape[1] // nz
    blk = part // ny
    for z in range(nz):
        term[...] = factor * lax.dot_general(
            tokens[:, z * part : (z + 1) * part],
            rows,
            (((0,), (0,)), ((), ())),
            preferred_element_type=F32,
        )
        for out, ks in zip(outs, ORDER):
            for i, k in enumerate(ks):
                at = pl.multiple_of(lax.rem(y + k, ny) * blk, blk)
                out[i, z] = term[pl.ds(at, blk), :].astype(BF16)


def rows_and_chunks(sizes, factor, where, mine, theirs, cot, cot_far, gain, tokens):
    nx, nh, ny, nz = sizes
    heads = mine.shape[1]
    part = tokens.shape[1] // nz
    vmem = pl.BlockSpec(memory_space=pltpu.VMEM)
    chunks = [jax.ShapeDtypeStruct((len(ks), nz, part // ny, heads), BF16) for ks in ORDER]
    return pl.pallas_call(
        functools.partial(rows_kernel, sizes, factor),
        out_shape=[jax.ShapeDtypeStruct(mine.shape, BF16)] + chunks,
        in_specs=[pl.BlockSpec(memory_space=pltpu.SMEM)] + [vmem] * 6,
        out_specs=[vmem] * (len(ORDER) + 1),
        scratch_shapes=[pltpu.VMEM((part, heads), F32)],
        compiler_params=pltpu.CompilerParams(vmem_limit_bytes=8 * 2**20),
        name="rows_and_chunks",
    )(where, mine, theirs, cot, cot_far, gain, tokens)


def small_call(kernel, out_shape, *operands, where=None):
    vmem = pl.BlockSpec(memory_space=pltpu.VMEM)
    scalars = () if where is None else (where,)
    return pl.pallas_call(
        kernel,
        out_shape=out_shape,
        in_specs=[pl.BlockSpec(memory_space=pltpu.SMEM)] * len(scalars) + [vmem] * len(operands),
        out_specs=[vmem] * len(out_shape),
        compiler_params=pltpu.CompilerParams(vmem_limit_bytes=8 * 2**20),
        cost_estimate=pl.CostEstimate(flops=0, transcendentals=0, bytes_accessed=0),
    )(*scalars, *operands)


def backs_kernel(rows, weight, *outs):
    count = outs[0].shape[0]
    for k, out in enumerate(outs):
        out[...] = lax.dot_general(
            rows[k * count : (k + 1) * count, :],
            weight[...],
            (((1,), (1,)), ((), ())),
            preferred_element_type=F32,
        ).astype(out.dtype)


def back_sum_kernel(first, *rest):
    terms, (near, far) = rest[:-2], rest[-2:]
    count = near.shape[0]
    for span, out in ((pl.ds(0, count), near), (pl.ds(count, count), far)):
        total = first[span, :]
        for t in terms:
            total = total + t[span, :].astype(F32)
        out[...] = total.astype(out.dtype)


def over_y_kernel(where, own, up, down, got2, got4, got6, kept, *sends):
    count, third = kept.shape[0], len(sends) + 1
    for k in range(third):
        place = lax.rem(where[0] + k, third)
        for i in range(count):
            z = i * third + place
            total = own[0, z].astype(F32) + got4[z].astype(F32)
            total = total + (up[1, z].astype(F32) + down[1, z].astype(F32))
            total = total + (got2[z].astype(F32) + got6[z].astype(F32))
            if k:
                sends[k - 1][i] = total.astype(BF16)
            else:
                kept[i] = total


def over_third_kernel(where, kept, *rest):
    got, (stay, send) = rest[:-2], rest[-2:]
    side = where[1]
    for at, out in ((side, stay), (1 - side, send)):
        total = kept[at]
        for g in got:
            total = total + g[at].astype(F32)
        out[...] = total.astype(out.dtype)


def shift(value, axis, by):
    size = lax.axis_size(axis)
    return lax.ppermute(value, axis, [(i, (i + by) % size) for i in range(size)])


def add(*terms):
    total = terms[0].astype(F32)
    for t in terms[1:]:
        total = total + t.astype(F32)
    return total


def body(normed, weight, cotangent, head_gain):
    nx, ny, nz, nh = (lax.axis_size(a) for a in ("x", "y", "zl", "zh"))
    count, width = normed.shape
    heads = weight.shape[1]
    where = jnp.stack([lax.axis_index(a) for a in ("x", "y")]).astype(jnp.int32)
    zh = lax.axis_index("zh")

    def mirror(value):
        ends = [(i, nz * nh - 1 - i) for i in range(nz * nh)]
        return lax.ppermute(value, ("zl", "zh"), ends)

    peer = mirror(normed)
    own = [normed] + [shift(normed, "x", k) for k in (1, 2, 3)]
    cot = cotangent.reshape(nx, nh, count, heads)
    cot_far = lax.dynamic_index_in_dim(cot, 1 - zh, 1, False)
    cot_far = lax.ppermute(cot_far, "zl", [(i, nz - 1 - i) for i in range(nz)])
    cot = lax.dynamic_index_in_dim(cot, zh, 1, False)
    peer, cot_far = lax.optimization_barrier((peer, cot_far))
    other = [peer] + [shift(peer, "x", k) for k in (1, 2, 3)]
    tokens = jnp.concatenate([p for pair in zip(own, other) for p in pair], axis=0)

    mine = jnp.dot(tokens, weight, preferred_element_type=F32)
    theirs = shift(mine, "c", 1)
    factor = 1.0 / math.sqrt(count * nx * nh * ny * nz)
    rows, *c = rows_and_chunks(
        (nx, nh, ny, nz),
        factor,
        where,
        mine,
        theirs,
        cot,
        cot_far,
        head_gain.reshape(1, -1),
        tokens,
    )

    up, down, across, two, six, own = c
    turn = [
        (i * 2 + j, (i + (4, -4)[j]) % ny * 2 + j) for i in range(ny) for j in range(2)
    ]
    got_up, got_down = shift(up, "y", 1), shift(down, "y", -1)
    got4 = lax.ppermute(across[0], ("y", "c"), turn)
    two = add(two[0], got_up[0]).astype(BF16)
    six = add(six[0], got_down[0]).astype(BF16)
    got2, got6 = shift(two, "y", 2), shift(six, "y", -2)

    block = (nh * count, width)
    back = small_call(
        backs_kernel,
        [jax.ShapeDtypeStruct(block, F32)] + [jax.ShapeDtypeStruct(block, BF16)] * (nx - 1),
        rows,
        weight,
    )
    near, far = small_call(
        back_sum_kernel,
        [jax.ShapeDtypeStruct((count, width), t) for t in (F32, BF16)],
        back[0],
        *[shift(back[k], "x", -k) for k in (2, 1, 3)],
    )
    input_grad = add(near, mirror(far)).astype(BF16)

    third = nz // 2
    zl = lax.axis_index("zl")
    spot = jnp.stack([zl % third, zl // third]).astype(jnp.int32)
    blk = own.shape[2]
    kept, *sends = small_call(
        over_y_kernel,
        [jax.ShapeDtypeStruct((2, blk, heads), t) for t in (F32, *[BF16] * (third - 1))],
        own,
        got_up,
        got_down,
        got2,
        got4,
        got6,
        where=spot,
    )
    got = []
    for k in range(1, third):
        hop = [(i, i // third * third + (i + k) % third) for i in range(nz)]
        got.append(lax.ppermute(sends[k - 1], "zl", hop))
    stay, send = small_call(
        over_third_kernel,
        [jax.ShapeDtypeStruct((blk, heads), t) for t in (F32, BF16)],
        kept,
        *got,
        where=spot,
    )
    weight_grad = add(stay, shift(send, "zl", third))
    return (input_grad, weight_grad)


def spread(fine):
    return jax.shard_map(
        body,
        mesh=fine,
        in_specs=(
            P(("zl", "y", "x", "zh"), "c"),
            P("c", ("x", "zh")),
            P(("zl", "y"), ("x", "zh")),
            P(),
        ),
        out_specs=(P(("zl", "y", "x", "zh"), "c"), P(("c", "zl", "y"), ("x", "zh"))),
        check_vma=False,
    )


def solution(mesh):
    return spread(Mesh(mesh.devices.reshape(6, 8, 4, 2, 2), ("zl", "y", "x", "zh", "c")))
```

```python
import functools
import math

import jax
import jax.numpy as jnp
from jax import lax
from jax.experimental import pallas as pl
from jax.experimental.pallas import tpu as pltpu
from jax.sharding import Mesh, PartitionSpec as P

F32 = jnp.float32
BF16 = jnp.bfloat16
ORDER = ((3, 1), (5, 7), (4,), (2,), (6,), (0,))


def mean(value):
    return jnp.mean(value, axis=-1, keepdims=True)


def rows_kernel(sizes, factor, where, mine, theirs, cot, cot_far, gain, tokens, rows_out, *rest):
    nx, nh, ny, nz = sizes
    outs, term = rest[:-1], rest[-1]
    x, y = where[0], where[1]
    count = cot.shape[1]
    heads = mine.shape[1]
    hd = gain.shape[1]
    for kh, side in enumerate((cot, cot_far)):
        for kx in range(nx):
            block = lax.rem(x - kx + nx, nx)
            span = pl.ds((kh * nx + kx) * count, count)
            for h in range(0, heads, hd):
                pre = mine[span, h : h + hd] + theirs[span, h : h + hd]
                centred = pre - mean(pre)
                inverse = lax.rsqrt(mean(centred * centred) + 1e-06)
                unit = centred * inverse
                scaled = side[block, :, h : h + hd].astype(F32) * gain[...]
                result = inverse * (scaled - mean(scaled) - unit * mean(scaled * unit))
                rows_out[span, h : h + hd] = result.astype(BF16)
    rows = rows_out[...]
    part = tokens.shape[1] // nz
    blk = part // ny
    for z in range(nz):
        term[...] = factor * lax.dot_general(
            tokens[:, z * part : (z + 1) * part],
            rows,
            (((0,), (0,)), ((), ())),
            preferred_element_type=F32,
        )
        for out, ks in zip(outs, ORDER):
            for i, k in enumerate(ks):
                at = pl.multiple_of(lax.rem(y + k, ny) * blk, blk)
                out[i, z] = term[pl.ds(at, blk), :].astype(BF16)


def rows_and_chunks(sizes, factor, where, mine, theirs, cot, cot_far, gain, tokens):
    nx, nh, ny, nz = sizes
    heads = mine.shape[1]
    part = tokens.shape[1] // nz
    vmem = pl.BlockSpec(memory_space=pltpu.VMEM)
    chunks = [jax.ShapeDtypeStruct((len(ks), nz, part // ny, heads), BF16) for ks in ORDER]
    return pl.pallas_call(
        functools.partial(rows_kernel, sizes, factor),
        out_shape=[jax.ShapeDtypeStruct(mine.shape, BF16)] + chunks,
        in_specs=[pl.BlockSpec(memory_space=pltpu.SMEM)] + [vmem] * 6,
        out_specs=[vmem] * (len(ORDER) + 1),
        scratch_shapes=[pltpu.VMEM((part, heads), F32)],
        compiler_params=pltpu.CompilerParams(vmem_limit_bytes=8 * 2**20),
        name="rows_and_chunks",
    )(where, mine, theirs, cot, cot_far, gain, tokens)


def small_call(kernel, out_shape, *operands, where=None):
    vmem = pl.BlockSpec(memory_space=pltpu.VMEM)
    scalars = () if where is None else (where,)
    return pl.pallas_call(
        kernel,
        out_shape=out_shape,
        in_specs=[pl.BlockSpec(memory_space=pltpu.SMEM)] * len(scalars) + [vmem] * len(operands),
        out_specs=[vmem] * len(out_shape),
        compiler_params=pltpu.CompilerParams(vmem_limit_bytes=8 * 2**20),
        cost_estimate=pl.CostEstimate(flops=0, transcendentals=0, bytes_accessed=0),
    )(*scalars, *operands)


def backs_kernel(base, rows, weight, *outs):
    count = outs[0].shape[0]
    for k, out in enumerate(outs):
        out[...] = lax.dot_general(
            rows[base + k * count : base + (k + 1) * count, :],
            weight[...],
            (((1,), (1,)), ((), ())),
            preferred_element_type=F32,
        ).astype(out.dtype)


def sum_kernel(*refs):
    total = refs[0][...].astype(F32)
    for t in refs[1:-1]:
        total = total + t[...].astype(F32)
    refs[-1][...] = total.astype(refs[-1].dtype)


def relay_kernel(where, two, six, up, down, across, out_two, out_six):
    core = where[0]
    from4 = across[...].astype(F32)
    keep = jnp.where(core == 0, 1.0, 0.0)
    out_two[...] = (two[0].astype(F32) + up[0].astype(F32) + keep * from4).astype(BF16)
    out_six[...] = (six[0].astype(F32) + down[0].astype(F32) + (1.0 - keep) * from4).astype(BF16)


def over_y_kernel(where, own, up, down, got2, got6, kept, *sends):
    count, third = kept.shape[0], len(sends) + 1
    for k in range(third):
        place = lax.rem(where[0] + k, third)
        for i in range(count):
            z = i * third + place
            total = own[0, z].astype(F32) + (up[1, z].astype(F32) + down[1, z].astype(F32))
            total = total + (got2[z].astype(F32) + got6[z].astype(F32))
            if k:
                sends[k - 1][i] = total.astype(BF16)
            else:
                kept[i] = total


def over_third_kernel(where, kept, *rest):
    got, (stay, send) = rest[:-2], rest[-2:]
    side = where[1]
    for at, out in ((side, stay), (1 - side, send)):
        total = kept[at]
        for g in got:
            total = total + g[at].astype(F32)
        out[...] = total.astype(out.dtype)


def shift(value, axis, by):
    size = lax.axis_size(axis)
    return lax.ppermute(value, axis, [(i, (i + by) % size) for i in range(size)])


def add(*terms):
    total = terms[0].astype(F32)
    for t in terms[1:]:
        total = total + t.astype(F32)
    return total


def body(normed, weight, cotangent, head_gain):
    nx, ny, nz, nh = (lax.axis_size(a) for a in ("x", "y", "zl", "zh"))
    count, width = normed.shape
    heads = weight.shape[1]
    where = jnp.stack([lax.axis_index(a) for a in ("x", "y")]).astype(jnp.int32)
    zh = lax.axis_index("zh")

    def mirror(value):
        ends = [(i, nz * nh - 1 - i) for i in range(nz * nh)]
        return lax.ppermute(value, ("zl", "zh"), ends)

    peer = mirror(normed)
    own = [normed] + [shift(normed, "x", k) for k in (1, 2, 3)]
    cot = cotangent.reshape(nx, nh, count, heads)
    cot_far = lax.dynamic_index_in_dim(cot, 1 - zh, 1, False)
    cot_far = lax.ppermute(cot_far, "zl", [(i, nz - 1 - i) for i in range(nz)])
    cot = lax.dynamic_index_in_dim(cot, zh, 1, False)
    peer, cot_far = lax.optimization_barrier((peer, cot_far))
    other = [peer] + [shift(peer, "x", k) for k in (1, 2, 3)]
    tokens = jnp.concatenate(own + other, axis=0)

    mine = jnp.dot(tokens, weight, preferred_element_type=F32)
    theirs = shift(mine, "c", 1)
    factor = 1.0 / math.sqrt(count * nx * nh * ny * nz)
    rows, *c = rows_and_chunks(
        (nx, nh, ny, nz),
        factor,
        where,
        mine,
        theirs,
        cot,
        cot_far,
        head_gain.reshape(1, -1),
        tokens,
    )

    up, down, across, two, six, own = c
    turn = [
        (i * 2 + j, (i + (2, -2)[j]) % ny * 2 + j) for i in range(ny) for j in range(2)
    ]
    got_up, got_down = shift(up, "y", 1), shift(down, "y", -1)
    got4 = lax.ppermute(across[0], ("y", "c"), turn)
    core = lax.axis_index("c").astype(jnp.int32).reshape(1)
    chunk = jax.ShapeDtypeStruct(got4.shape, BF16)
    relay = small_call(
        relay_kernel, [chunk, chunk], two, six, got_up, got_down, got4, where=core
    )

    block = (count, width)

    def over_x(rows, base):
        back = small_call(
            functools.partial(backs_kernel, base),
            [jax.ShapeDtypeStruct(block, F32)] + [jax.ShapeDtypeStruct(block, BF16)] * (nx - 1),
            rows,
            weight,
        )
        return [back[0]] + [shift(back[k], "x", -k) for k in (2, 1, 3)]

    total = jax.ShapeDtypeStruct(block, BF16)
    far = small_call(sum_kernel, [total], *over_x(rows, nx * count))[0]
    rows, two, six = lax.optimization_barrier((rows, *relay))
    got2, got6 = shift(two, "y", 2), shift(six, "y", -2)
    near = over_x(rows, 0)
    far = mirror(far)

    third = nz // 2
    zl = lax.axis_index("zl")
    spot = jnp.stack([zl % third, zl // third]).astype(jnp.int32)
    blk = own.shape[2]
    kept, *sends = small_call(
        over_y_kernel,
        [jax.ShapeDtypeStruct((2, blk, heads), t) for t in (F32, *[BF16] * (third - 1))],
        own,
        got_up,
        got_down,
        got2,
        got6,
        where=spot,
    )
    near[1], *sends = lax.optimization_barrier((near[1], *sends))
    got = []
    for k in range(1, third):
        hop = [(i, i // third * third + (i + k) % third) for i in range(nz)]
        got.append(lax.ppermute(sends[k - 1], "zl", hop))
    stay, send = small_call(
        over_third_kernel,
        [jax.ShapeDtypeStruct((blk, heads), t) for t in (F32, BF16)],
        kept,
        *got,
        where=spot,
    )
    input_grad = small_call(sum_kernel, [total], *near, far)[0]
    weight_grad = add(stay, shift(send, "zl", third))
    return (input_grad, weight_grad)


def spread(fine):
    return jax.shard_map(
        body,
        mesh=fine,
        in_specs=(
            P(("zl", "y", "x", "zh"), "c"),
            P("c", ("x", "zh")),
            P(("zl", "y"), ("x", "zh")),
            P(),
        ),
        out_specs=(P(("zl", "y", "x", "zh"), "c"), P(("c", "zl", "y"), ("x", "zh"))),
        check_vma=False,
    )


def solution(mesh):
    return spread(Mesh(mesh.devices.reshape(6, 8, 4, 2, 2), ("zl", "y", "x", "zh", "c")))
```

```python
import functools
import math

import jax
import jax.numpy as jnp
from jax import lax
from jax.experimental import pallas as pl
from jax.experimental.pallas import tpu as pltpu
from jax.sharding import Mesh, PartitionSpec as P

F32 = jnp.float32
BF16 = jnp.bfloat16
ORDER = ((3, 1), (5, 7), (4,), (2,), (6,), (0,))


def mean(value):
    return jnp.mean(value, axis=-1, keepdims=True)


def rows_kernel(sizes, factor, where, mine, theirs, cot, cot_far, gain, tokens, rows_out, *rest):
    nx, nh, ny, nz = sizes
    outs, term = rest[:-1], rest[-1]
    x, y = where[0], where[1]
    count = cot.shape[1]
    heads = mine.shape[1]
    hd = gain.shape[1]
    for kx in range(nx):
        block = lax.rem(x - kx + nx, nx)
        for kh in range(nh):
            span = pl.ds((kx * nh + kh) * count, count)
            side = (cot, cot_far)[kh]
            for h in range(0, heads, hd):
                pre = mine[span, h : h + hd] + theirs[span, h : h + hd]
                centred = pre - mean(pre)
                inverse = lax.rsqrt(mean(centred * centred) + 1e-06)
                unit = centred * inverse
                scaled = side[block, :, h : h + hd].astype(F32) * gain[...]
                result = inverse * (scaled - mean(scaled) - unit * mean(scaled * unit))
                rows_out[span, h : h + hd] = result.astype(BF16)
    rows = rows_out[...]
    part = tokens.shape[1] // nz
    blk = part // ny
    for z in range(nz):
        term[...] = factor * lax.dot_general(
            tokens[:, z * part : (z + 1) * part],
            rows,
            (((0,), (0,)), ((), ())),
            preferred_element_type=F32,
        )
        for out, ks in zip(outs, ORDER):
            for i, k in enumerate(ks):
                at = pl.multiple_of(lax.rem(y + k, ny) * blk, blk)
                out[i, z] = term[pl.ds(at, blk), :].astype(BF16)


def rows_and_chunks(sizes, factor, where, mine, theirs, cot, cot_far, gain, tokens):
    nx, nh, ny, nz = sizes
    heads = mine.shape[1]
    part = tokens.shape[1] // nz
    vmem = pl.BlockSpec(memory_space=pltpu.VMEM)
    chunks = [jax.ShapeDtypeStruct((len(ks), nz, part // ny, heads), BF16) for ks in ORDER]
    return pl.pallas_call(
        functools.partial(rows_kernel, sizes, factor),
        out_shape=[jax.ShapeDtypeStruct(mine.shape, BF16)] + chunks,
        in_specs=[pl.BlockSpec(memory_space=pltpu.SMEM)] + [vmem] * 6,
        out_specs=[vmem] * (len(ORDER) + 1),
        scratch_shapes=[pltpu.VMEM((part, heads), F32)],
        compiler_params=pltpu.CompilerParams(vmem_limit_bytes=8 * 2**20),
        name="rows_and_chunks",
    )(where, mine, theirs, cot, cot_far, gain, tokens)


def small_call(kernel, out_shape, *operands, where=None):
    vmem = pl.BlockSpec(memory_space=pltpu.VMEM)
    scalars = () if where is None else (where,)
    return pl.pallas_call(
        kernel,
        out_shape=out_shape,
        in_specs=[pl.BlockSpec(memory_space=pltpu.SMEM)] * len(scalars) + [vmem] * len(operands),
        out_specs=[vmem] * len(out_shape),
        compiler_params=pltpu.CompilerParams(vmem_limit_bytes=8 * 2**20),
        cost_estimate=pl.CostEstimate(flops=0, transcendentals=0, bytes_accessed=0),
    )(*scalars, *operands)


def backs_kernel(rows, weight, *outs):
    count = outs[0].shape[0]
    for k, out in enumerate(outs):
        out[...] = lax.dot_general(
            rows[k * count : (k + 1) * count, :],
            weight[...],
            (((1,), (1,)), ((), ())),
            preferred_element_type=F32,
        ).astype(out.dtype)


def back_sum_kernel(first, *rest):
    terms, (near, far) = rest[:-2], rest[-2:]
    count = near.shape[0]
    for span, out in ((pl.ds(0, count), near), (pl.ds(count, count), far)):
        total = first[span, :]
        for t in terms:
            total = total + t[span, :].astype(F32)
        out[...] = total.astype(out.dtype)


def relay_kernel(where, two, six, up, down, across, out_two, out_six):
    keep = jnp.where(where[0] == 0, 1.0, 0.0)
    from4 = across[...].astype(F32)
    out_two[...] = (two[0].astype(F32) + up[0].astype(F32) + keep * from4).astype(BF16)
    out_six[...] = (six[0].astype(F32) + down[0].astype(F32) + (1.0 - keep) * from4).astype(BF16)


def over_y_kernel(where, own, up, down, got2, got6, kept, *sends):
    count, third = kept.shape[0], len(sends) + 1
    for k in range(third):
        place = lax.rem(where[0] + k, third)
        for i in range(count):
            z = i * third + place
            total = own[0, z].astype(F32) + (up[1, z].astype(F32) + down[1, z].astype(F32))
            total = total + (got2[z].astype(F32) + got6[z].astype(F32))
            if k:
                sends[k - 1][i] = total.astype(BF16)
            else:
                kept[i] = total


def over_third_kernel(where, kept, *rest):
    got, (stay, send) = rest[:-2], rest[-2:]
    side = where[1]
    for at, out in ((side, stay), (1 - side, send)):
        total = kept[at]
        for g in got:
            total = total + g[at].astype(F32)
        out[...] = total.astype(out.dtype)


def shift(value, axis, by):
    size = lax.axis_size(axis)
    return lax.ppermute(value, axis, [(i, (i + by) % size) for i in range(size)])


def add(*terms):
    total = terms[0].astype(F32)
    for t in terms[1:]:
        total = total + t.astype(F32)
    return total


def body(normed, weight, cotangent, head_gain):
    nx, ny, nz, nh = (lax.axis_size(a) for a in ("x", "y", "zl", "zh"))
    count, width = normed.shape
    heads = weight.shape[1]
    where = jnp.stack([lax.axis_index(a) for a in ("x", "y")]).astype(jnp.int32)
    zh = lax.axis_index("zh")

    def mirror(value):
        ends = [(i, nz * nh - 1 - i) for i in range(nz * nh)]
        return lax.ppermute(value, ("zl", "zh"), ends)

    peer = mirror(normed)
    own = [normed] + [shift(normed, "x", k) for k in (1, 2, 3)]
    cot = cotangent.reshape(nx, nh, count, heads)
    cot_far = lax.dynamic_index_in_dim(cot, 1 - zh, 1, False)
    cot_far = lax.ppermute(cot_far, "zl", [(i, nz - 1 - i) for i in range(nz)])
    cot = lax.dynamic_index_in_dim(cot, zh, 1, False)
    peer, cot_far = lax.optimization_barrier((peer, cot_far))
    other = [peer] + [shift(peer, "x", k) for k in (1, 2, 3)]
    tokens = jnp.concatenate([p for pair in zip(own, other) for p in pair], axis=0)

    mine = jnp.dot(tokens, weight, preferred_element_type=F32)
    theirs = shift(mine, "c", 1)
    factor = 1.0 / math.sqrt(count * nx * nh * ny * nz)
    rows, *c = rows_and_chunks(
        (nx, nh, ny, nz),
        factor,
        where,
        mine,
        theirs,
        cot,
        cot_far,
        head_gain.reshape(1, -1),
        tokens,
    )

    up, down, across, two, six, own = c
    turn = [
        (i * 2 + j, (i + (2, -2)[j]) % ny * 2 + j) for i in range(ny) for j in range(2)
    ]
    got_up, got_down = shift(up, "y", 1), shift(down, "y", -1)
    got4 = lax.ppermute(across[0], ("y", "c"), turn)
    core = lax.axis_index("c").astype(jnp.int32).reshape(1)
    chunk = jax.ShapeDtypeStruct(got4.shape, BF16)
    two, six = small_call(
        relay_kernel, [chunk, chunk], two, six, got_up, got_down, got4, where=core
    )
    got2, got6 = shift(two, "y", 2), shift(six, "y", -2)

    block = (nh * count, width)
    back = small_call(
        backs_kernel,
        [jax.ShapeDtypeStruct(block, F32)] + [jax.ShapeDtypeStruct(block, BF16)] * (nx - 1),
        rows,
        weight,
    )
    near, far = small_call(
        back_sum_kernel,
        [jax.ShapeDtypeStruct((count, width), t) for t in (F32, BF16)],
        back[0],
        *[shift(back[k], "x", -k) for k in (2, 1, 3)],
    )
    input_grad = add(near, mirror(far)).astype(BF16)

    third = nz // 2
    zl = lax.axis_index("zl")
    spot = jnp.stack([zl % third, zl // third]).astype(jnp.int32)
    blk = own.shape[2]
    kept, *sends = small_call(
        over_y_kernel,
        [jax.ShapeDtypeStruct((2, blk, heads), t) for t in (F32, *[BF16] * (third - 1))],
        own,
        got_up,
        got_down,
        got2,
        got6,
        where=spot,
    )
    got = []
    for k in range(1, third):
        hop = [(i, i // third * third + (i + k) % third) for i in range(nz)]
        got.append(lax.ppermute(sends[k - 1], "zl", hop))
    stay, send = small_call(
        over_third_kernel,
        [jax.ShapeDtypeStruct((blk, heads), t) for t in (F32, BF16)],
        kept,
        *got,
        where=spot,
    )
    weight_grad = add(stay, shift(send, "zl", third))
    return (input_grad, weight_grad)


def spread(fine):
    return jax.shard_map(
        body,
        mesh=fine,
        in_specs=(
            P(("zl", "y", "x", "zh"), "c"),
            P("c", ("x", "zh")),
            P(("zl", "y"), ("x", "zh")),
            P(),
        ),
        out_specs=(P(("zl", "y", "x", "zh"), "c"), P(("c", "zl", "y"), ("x", "zh"))),
        check_vma=False,
    )


def solution(mesh):
    return spread(Mesh(mesh.devices.reshape(6, 8, 4, 2, 2), ("zl", "y", "x", "zh", "c")))
```

```python
import functools
import math

import jax
import jax.numpy as jnp
from jax import lax
from jax.experimental import pallas as pl
from jax.experimental.pallas import tpu as pltpu
from jax.sharding import Mesh, PartitionSpec as P

F32 = jnp.float32
BF16 = jnp.bfloat16
ORDER = (
    ((1, 0), (1, 1), (6, 0), (6, 1), (4, 0)),
    ((7, 0), (7, 1), (2, 0), (2, 1), (4, 1)),
    ((3, 0), (3, 1)),
    ((5, 0), (5, 1)),
    ((0, 0), (0, 1)),
)


def mean(value):
    return jnp.mean(value, axis=-1, keepdims=True)


def rows_kernel(sizes, factor, where, mine, theirs, cot, cot_far, gain, tokens, rows_out, *rest):
    nx, nh, ny, nz = sizes
    outs, term = rest[:-1], rest[-1]
    x, y = where[0], where[1]
    count = cot.shape[1]
    heads = mine.shape[1]
    hd = gain.shape[1]
    for kx in range(nx):
        block = lax.rem(x - kx + nx, nx)
        for kh in range(nh):
            span = pl.ds((kx * nh + kh) * count, count)
            side = (cot, cot_far)[kh]
            for h in range(0, heads, hd):
                pre = mine[span, h : h + hd] + theirs[span, h : h + hd]
                centred = pre - mean(pre)
                inverse = lax.rsqrt(mean(centred * centred) + 1e-06)
                unit = centred * inverse
                scaled = side[block, :, h : h + hd].astype(F32) * gain[...]
                result = inverse * (scaled - mean(scaled) - unit * mean(scaled * unit))
                rows_out[span, h : h + hd] = result.astype(BF16)
    rows = rows_out[...]
    part = tokens.shape[1] // nz
    blk = part // ny
    half = blk // 2
    for z in range(nz):
        term[...] = factor * lax.dot_general(
            tokens[:, z * part : (z + 1) * part],
            rows,
            (((0,), (0,)), ((), ())),
            preferred_element_type=F32,
        )
        for out, ks in zip(outs, ORDER):
            for i, (k, h) in enumerate(ks):
                at = pl.multiple_of(lax.rem(y + k, ny) * blk + h * half, half)
                out[i, z] = term[pl.ds(at, half), :].astype(BF16)


def rows_and_chunks(sizes, factor, where, mine, theirs, cot, cot_far, gain, tokens):
    nx, nh, ny, nz = sizes
    heads = mine.shape[1]
    part = tokens.shape[1] // nz
    vmem = pl.BlockSpec(memory_space=pltpu.VMEM)
    chunks = [jax.ShapeDtypeStruct((len(ks), nz, part // ny // 2, heads), BF16) for ks in ORDER]
    return pl.pallas_call(
        functools.partial(rows_kernel, sizes, factor),
        out_shape=[jax.ShapeDtypeStruct(mine.shape, BF16)] + chunks,
        in_specs=[pl.BlockSpec(memory_space=pltpu.SMEM)] + [vmem] * 6,
        out_specs=[vmem] * (len(ORDER) + 1),
        scratch_shapes=[pltpu.VMEM((part, heads), F32)],
        compiler_params=pltpu.CompilerParams(vmem_limit_bytes=8 * 2**20),
        name="rows_and_chunks",
    )(where, mine, theirs, cot, cot_far, gain, tokens)


def small_call(kernel, out_shape, *operands, where=None):
    vmem = pl.BlockSpec(memory_space=pltpu.VMEM)
    scalars = () if where is None else (where,)
    return pl.pallas_call(
        kernel,
        out_shape=out_shape,
        in_specs=[pl.BlockSpec(memory_space=pltpu.SMEM)] * len(scalars) + [vmem] * len(operands),
        out_specs=[vmem] * len(out_shape),
        compiler_params=pltpu.CompilerParams(vmem_limit_bytes=8 * 2**20),
        cost_estimate=pl.CostEstimate(flops=0, transcendentals=0, bytes_accessed=0),
    )(*scalars, *operands)


def backs_kernel(rows, weight, *outs):
    count = outs[0].shape[0]
    for k, out in enumerate(outs):
        out[...] = lax.dot_general(
            rows[k * count : (k + 1) * count, :],
            weight[...],
            (((1,), (1,)), ((), ())),
            preferred_element_type=F32,
        ).astype(out.dtype)


def back_sum_kernel(first, *rest):
    terms, (near, far) = rest[:-2], rest[-2:]
    count = near.shape[0]
    for span, out in ((pl.ds(0, count), near), (pl.ds(count, count), far)):
        total = first[span, :]
        for t in terms:
            total = total + t[span, :].astype(F32)
        out[...] = total.astype(out.dtype)


def over_y_kernel(where, own, up, down, got3, got5, kept, *sends):
    count, third = kept.shape[0], len(sends) + 1
    half = own.shape[2]
    for k in range(third):
        place = lax.rem(where[0] + k, third)
        for i in range(count):
            z = i * third + place
            for h in range(2):
                total = own[h, z].astype(F32) + (up[h, z].astype(F32) + down[h, z].astype(F32))
                total = total + (got3[h, z].astype(F32) + got5[h, z].astype(F32))
                out = sends[k - 1] if k else kept
                out[i, h * half : (h + 1) * half] = total.astype(out.dtype)


def over_third_kernel(where, kept, *rest):
    got, (stay, send) = rest[:-2], rest[-2:]
    side = where[1]
    for at, out in ((side, stay), (1 - side, send)):
        total = kept[at]
        for g in got:
            total = total + g[at].astype(F32)
        out[...] = total.astype(out.dtype)


def shift(value, axis, by):
    size = lax.axis_size(axis)
    return lax.ppermute(value, axis, [(i, (i + by) % size) for i in range(size)])


def add(*terms):
    total = terms[0].astype(F32)
    for t in terms[1:]:
        total = total + t.astype(F32)
    return total


def body(normed, weight, cotangent, head_gain):
    nx, ny, nz, nh = (lax.axis_size(a) for a in ("x", "y", "zl", "zh"))
    count, width = normed.shape
    heads = weight.shape[1]
    where = jnp.stack([lax.axis_index(a) for a in ("x", "y")]).astype(jnp.int32)
    zh = lax.axis_index("zh")

    def mirror(value):
        ends = [(i, nz * nh - 1 - i) for i in range(nz * nh)]
        return lax.ppermute(value, ("zl", "zh"), ends)

    peer = mirror(normed)
    own = [normed] + [shift(normed, "x", k) for k in (1, 2, 3)]
    cot = cotangent.reshape(nx, nh, count, heads)
    cot_far = lax.dynamic_index_in_dim(cot, 1 - zh, 1, False)
    cot_far = lax.ppermute(cot_far, "zl", [(i, nz - 1 - i) for i in range(nz)])
    cot = lax.dynamic_index_in_dim(cot, zh, 1, False)
    peer, cot_far = lax.optimization_barrier((peer, cot_far))
    other = [peer] + [shift(peer, "x", k) for k in (1, 2, 3)]
    tokens = jnp.concatenate([p for pair in zip(own, other) for p in pair], axis=0)

    mine = jnp.dot(tokens, weight, preferred_element_type=F32)
    theirs = shift(mine, "c", 1)
    factor = 1.0 / math.sqrt(count * nx * nh * ny * nz)
    rows, *c = rows_and_chunks(
        (nx, nh, ny, nz),
        factor,
        where,
        mine,
        theirs,
        cot,
        cot_far,
        head_gain.reshape(1, -1),
        tokens,
    )

    up, down, three, five, own = c
    got_up, got_down = shift(up, "y", 1), shift(down, "y", -1)
    low = jnp.pad(got_up[4:].astype(F32), ((0, 1), (0, 0), (0, 0), (0, 0)))
    high = jnp.pad(got_down[4:].astype(F32), ((1, 0), (0, 0), (0, 0), (0, 0)))
    three = add(three, got_down[2:4], low).astype(BF16)
    five = add(five, got_up[2:4], high).astype(BF16)
    got3, got5 = shift(three, "y", 3), shift(five, "y", -3)

    block = (nh * count, width)
    back = small_call(
        backs_kernel,
        [jax.ShapeDtypeStruct(block, F32)] + [jax.ShapeDtypeStruct(block, BF16)] * (nx - 1),
        rows,
        weight,
    )
    near, far = small_call(
        back_sum_kernel,
        [jax.ShapeDtypeStruct((count, width), t) for t in (F32, BF16)],
        back[0],
        *[shift(back[k], "x", -k) for k in (2, 1, 3)],
    )
    input_grad = add(near, mirror(far)).astype(BF16)

    third = nz // 2
    zl = lax.axis_index("zl")
    spot = jnp.stack([zl % third, zl // third]).astype(jnp.int32)
    blk = 2 * own.shape[2]
    kept, *sends = small_call(
        over_y_kernel,
        [jax.ShapeDtypeStruct((2, blk, heads), t) for t in (F32, *[BF16] * (third - 1))],
        own,
        got_up,
        got_down,
        got3,
        got5,
        where=spot,
    )
    got = []
    for k in range(1, third):
        hop = [(i, i // third * third + (i + k) % third) for i in range(nz)]
        got.append(lax.ppermute(sends[k - 1], "zl", hop))
    stay, send = small_call(
        over_third_kernel,
        [jax.ShapeDtypeStruct((blk, heads), t) for t in (F32, BF16)],
        kept,
        *got,
        where=spot,
    )
    weight_grad = add(stay, shift(send, "zl", third))
    return (input_grad, weight_grad)


def spread(fine):
    return jax.shard_map(
        body,
        mesh=fine,
        in_specs=(
            P(("zl", "y", "x", "zh"), "c"),
            P("c", ("x", "zh")),
            P(("zl", "y"), ("x", "zh")),
            P(),
        ),
        out_specs=(P(("zl", "y", "x", "zh"), "c"), P(("c", "zl", "y"), ("x", "zh"))),
        check_vma=False,
    )


def solution(mesh):
    return spread(Mesh(mesh.devices.reshape(6, 8, 4, 2, 2), ("zl", "y", "x", "zh", "c")))
```

```python
import functools
import math

import jax
import jax.numpy as jnp
from jax import lax
from jax.experimental import pallas as pl
from jax.experimental.pallas import tpu as pltpu
from jax.sharding import Mesh, PartitionSpec as P

F32 = jnp.float32
BF16 = jnp.bfloat16
ORDER = (
    ((1, 0), (1, 1), (6, 0), (6, 1), (4, 0)),
    ((7, 0), (7, 1), (2, 0), (2, 1), (4, 1)),
    ((3, 0), (3, 1)),
    ((5, 0), (5, 1)),
    ((0, 0), (0, 1)),
)


def mean(value):
    return jnp.mean(value, axis=-1, keepdims=True)


def rows_kernel(sizes, factor, where, mine, theirs, cot, cot_far, gain, tokens, rows_out, *rest):
    nx, nh, ny, nz = sizes
    outs, term = rest[:-1], rest[-1]
    x, y = where[0], where[1]
    count = cot.shape[1]
    heads = mine.shape[1]
    hd = gain.shape[1]
    for kx in range(nx):
        block = lax.rem(x - kx + nx, nx)
        for kh in range(nh):
            span = pl.ds((kx * nh + kh) * count, count)
            side = (cot, cot_far)[kh]
            for h in range(0, heads, hd):
                pre = mine[span, h : h + hd] + theirs[span, h : h + hd]
                centred = pre - mean(pre)
                inverse = lax.rsqrt(mean(centred * centred) + 1e-06)
                unit = centred * inverse
                scaled = side[block, :, h : h + hd].astype(F32) * gain[...]
                result = inverse * (scaled - mean(scaled) - unit * mean(scaled * unit))
                rows_out[span, h : h + hd] = result.astype(BF16)
    rows = rows_out[...]
    part = tokens.shape[1] // nz
    blk = part // ny
    half = blk // 2
    for z in range(nz):
        term[...] = factor * lax.dot_general(
            tokens[:, z * part : (z + 1) * part],
            rows,
            (((0,), (0,)), ((), ())),
            preferred_element_type=F32,
        )
        for out, ks in zip(outs, ORDER):
            for i, (k, h) in enumerate(ks):
                at = pl.multiple_of(lax.rem(y + k, ny) * blk + h * half, half)
                out[i, z] = term[pl.ds(at, half), :].astype(BF16)


def rows_and_chunks(sizes, factor, where, mine, theirs, cot, cot_far, gain, tokens):
    nx, nh, ny, nz = sizes
    heads = mine.shape[1]
    part = tokens.shape[1] // nz
    vmem = pl.BlockSpec(memory_space=pltpu.VMEM)
    chunks = [jax.ShapeDtypeStruct((len(ks), nz, part // ny // 2, heads), BF16) for ks in ORDER]
    return pl.pallas_call(
        functools.partial(rows_kernel, sizes, factor),
        out_shape=[jax.ShapeDtypeStruct(mine.shape, BF16)] + chunks,
        in_specs=[pl.BlockSpec(memory_space=pltpu.SMEM)] + [vmem] * 6,
        out_specs=[vmem] * (len(ORDER) + 1),
        scratch_shapes=[pltpu.VMEM((part, heads), F32)],
        compiler_params=pltpu.CompilerParams(vmem_limit_bytes=8 * 2**20),
        name="rows_and_chunks",
    )(where, mine, theirs, cot, cot_far, gain, tokens)


def small_call(kernel, out_shape, *operands, where=None):
    vmem = pl.BlockSpec(memory_space=pltpu.VMEM)
    scalars = () if where is None else (where,)
    return pl.pallas_call(
        kernel,
        out_shape=out_shape,
        in_specs=[pl.BlockSpec(memory_space=pltpu.SMEM)] * len(scalars) + [vmem] * len(operands),
        out_specs=[vmem] * len(out_shape),
        compiler_params=pltpu.CompilerParams(vmem_limit_bytes=8 * 2**20),
        cost_estimate=pl.CostEstimate(flops=0, transcendentals=0, bytes_accessed=0),
    )(*scalars, *operands)


def backs_kernel(rows, weight, *outs):
    count = outs[0].shape[0]
    for k, out in enumerate(outs):
        out[...] = lax.dot_general(
            rows[k * count : (k + 1) * count, :],
            weight[...],
            (((1,), (1,)), ((), ())),
            preferred_element_type=F32,
        ).astype(out.dtype)


def back_sum_kernel(first, *rest):
    terms, (near, far) = rest[:-2], rest[-2:]
    count = near.shape[0]
    for span, out in ((pl.ds(0, count), near), (pl.ds(count, count), far)):
        total = first[span, :]
        for t in terms:
            total = total + t[span, :].astype(F32)
        out[...] = total.astype(out.dtype)


def over_y_kernel(where, own, up, down, got3, got5, kept, *sends):
    count, third = kept.shape[0], len(sends) + 1
    half = own.shape[2]
    for k in range(third):
        place = lax.rem(where[0] + k, third)
        for i in range(count):
            z = i * third + place
            for h in range(2):
                total = own[h, z].astype(F32) + (up[h, z].astype(F32) + down[h, z].astype(F32))
                total = total + (got3[h, z].astype(F32) + got5[h, z].astype(F32))
                out = sends[k - 1] if k else kept
                out[i, h * half : (h + 1) * half] = total.astype(out.dtype)


def over_third_kernel(where, kept, *rest):
    got, (stay, send) = rest[:-2], rest[-2:]
    side = where[1]
    for at, out in ((side, stay), (1 - side, send)):
        total = kept[at]
        for g in got:
            total = total + g[at].astype(F32)
        out[...] = total.astype(out.dtype)


def shift(value, axis, by):
    size = lax.axis_size(axis)
    return lax.ppermute(value, axis, [(i, (i + by) % size) for i in range(size)])


def add(*terms):
    total = terms[0].astype(F32)
    for t in terms[1:]:
        total = total + t.astype(F32)
    return total


def body(normed, weight, cotangent, head_gain):
    nx, ny, nz, nh = (lax.axis_size(a) for a in ("x", "y", "zl", "zh"))
    count, width = normed.shape
    heads = weight.shape[1]
    where = jnp.stack([lax.axis_index(a) for a in ("x", "y")]).astype(jnp.int32)
    zh = lax.axis_index("zh")

    def mirror(value):
        ends = [(i, nz * nh - 1 - i) for i in range(nz * nh)]
        return lax.ppermute(value, ("zl", "zh"), ends)

    peer = mirror(normed)
    own = [normed] + [shift(normed, "x", k) for k in (1, 2, 3)]
    cot = cotangent.reshape(nx, nh, count, heads)
    cot_far = lax.dynamic_index_in_dim(cot, 1 - zh, 1, False)
    cot_far = lax.ppermute(cot_far, "zl", [(i, nz - 1 - i) for i in range(nz)])
    cot = lax.dynamic_index_in_dim(cot, zh, 1, False)
    other = [peer] + [shift(peer, "x", k) for k in (1, 2, 3)]
    other[2], cot_far = lax.optimization_barrier((other[2], cot_far))
    tokens = jnp.concatenate([p for pair in zip(own, other) for p in pair], axis=0)

    mine = jnp.dot(tokens, weight, preferred_element_type=F32)
    theirs = shift(mine, "c", 1)
    factor = 1.0 / math.sqrt(count * nx * nh * ny * nz)
    rows, *c = rows_and_chunks(
        (nx, nh, ny, nz),
        factor,
        where,
        mine,
        theirs,
        cot,
        cot_far,
        head_gain.reshape(1, -1),
        tokens,
    )

    up, down, three, five, own = c
    got_up, got_down = shift(up, "y", 1), shift(down, "y", -1)
    low = jnp.pad(got_up[4:].astype(F32), ((0, 1), (0, 0), (0, 0), (0, 0)))
    high = jnp.pad(got_down[4:].astype(F32), ((1, 0), (0, 0), (0, 0), (0, 0)))
    three = add(three, got_down[2:4], low).astype(BF16)
    five = add(five, got_up[2:4], high).astype(BF16)
    got3, got5 = shift(three, "y", 3), shift(five, "y", -3)

    block = (nh * count, width)
    back = small_call(
        backs_kernel,
        [jax.ShapeDtypeStruct(block, F32)] + [jax.ShapeDtypeStruct(block, BF16)] * (nx - 1),
        rows,
        weight,
    )
    near, far = small_call(
        back_sum_kernel,
        [jax.ShapeDtypeStruct((count, width), t) for t in (F32, BF16)],
        back[0],
        *[shift(back[k], "x", -k) for k in (2, 1, 3)],
    )
    input_grad = add(near, mirror(far)).astype(BF16)

    third = nz // 2
    zl = lax.axis_index("zl")
    spot = jnp.stack([zl % third, zl // third]).astype(jnp.int32)
    blk = 2 * own.shape[2]
    kept, *sends = small_call(
        over_y_kernel,
        [jax.ShapeDtypeStruct((2, blk, heads), t) for t in (F32, *[BF16] * (third - 1))],
        own,
        got_up,
        got_down,
        got3,
        got5,
        where=spot,
    )
    got = []
    for k in range(1, third):
        hop = [(i, i // third * third + (i + k) % third) for i in range(nz)]
        got.append(lax.ppermute(sends[k - 1], "zl", hop))
    stay, send = small_call(
        over_third_kernel,
        [jax.ShapeDtypeStruct((blk, heads), t) for t in (F32, BF16)],
        kept,
        *got,
        where=spot,
    )
    weight_grad = add(stay, shift(send, "zl", third))
    return (input_grad, weight_grad)


def spread(fine):
    return jax.shard_map(
        body,
        mesh=fine,
        in_specs=(
            P(("zl", "y", "x", "zh"), "c"),
            P("c", ("x", "zh")),
            P(("zl", "y"), ("x", "zh")),
            P(),
        ),
        out_specs=(P(("zl", "y", "x", "zh"), "c"), P(("c", "zl", "y"), ("x", "zh"))),
        check_vma=False,
    )


def solution(mesh):
    return spread(Mesh(mesh.devices.reshape(6, 8, 4, 2, 2), ("zl", "y", "x", "zh", "c")))
```

```python
import functools
import math

import jax
import jax.numpy as jnp
from jax import lax
from jax.experimental import pallas as pl
from jax.experimental.pallas import tpu as pltpu
from jax.sharding import Mesh, PartitionSpec as P

F32 = jnp.float32
BF16 = jnp.bfloat16
ORDER = (
    ((1, 0), (1, 1), (6, 0), (6, 1), (4, 0)),
    ((7, 0), (7, 1), (2, 0), (2, 1), (4, 1)),
    ((3, 0), (3, 1)),
    ((5, 0), (5, 1)),
    ((0, 0), (0, 1)),
)


def mean(value):
    return jnp.mean(value, axis=-1, keepdims=True)


def rows_kernel(sizes, factor, where, mine, theirs, cot, cot_far, gain, tokens, rows_out, *rest):
    nx, nh, ny, nz = sizes
    outs, term = rest[:-1], rest[-1]
    x, y = where[0], where[1]
    count = cot.shape[1]
    heads = mine.shape[1]
    hd = gain.shape[1]
    for kx in range(nx):
        block = lax.rem(x - kx + nx, nx)
        for kh in range(nh):
            span = pl.ds((kx * nh + kh) * count, count)
            side = (cot, cot_far)[kh]
            for h in range(0, heads, hd):
                pre = mine[span, h : h + hd] + theirs[span, h : h + hd]
                centred = pre - mean(pre)
                inverse = lax.rsqrt(mean(centred * centred) + 1e-06)
                unit = centred * inverse
                scaled = side[block, :, h : h + hd].astype(F32) * gain[...]
                result = inverse * (scaled - mean(scaled) - unit * mean(scaled * unit))
                rows_out[span, h : h + hd] = result.astype(BF16)
    rows = rows_out[...]
    part = tokens.shape[1] // nz
    blk = part // ny
    half = blk // 2
    for z in range(nz):
        term[...] = factor * lax.dot_general(
            tokens[:, z * part : (z + 1) * part],
            rows,
            (((0,), (0,)), ((), ())),
            preferred_element_type=F32,
        )
        for out, ks in zip(outs, ORDER):
            for i, (k, h) in enumerate(ks):
                at = pl.multiple_of(lax.rem(y + k, ny) * blk + h * half, half)
                out[i, z] = term[pl.ds(at, half), :].astype(BF16)


def rows_and_chunks(sizes, factor, where, mine, theirs, cot, cot_far, gain, tokens):
    nx, nh, ny, nz = sizes
    heads = mine.shape[1]
    part = tokens.shape[1] // nz
    vmem = pl.BlockSpec(memory_space=pltpu.VMEM)
    chunks = [jax.ShapeDtypeStruct((len(ks), nz, part // ny // 2, heads), BF16) for ks in ORDER]
    return pl.pallas_call(
        functools.partial(rows_kernel, sizes, factor),
        out_shape=[jax.ShapeDtypeStruct(mine.shape, BF16)] + chunks,
        in_specs=[pl.BlockSpec(memory_space=pltpu.SMEM)] + [vmem] * 6,
        out_specs=[vmem] * (len(ORDER) + 1),
        scratch_shapes=[pltpu.VMEM((part, heads), F32)],
        compiler_params=pltpu.CompilerParams(vmem_limit_bytes=8 * 2**20),
        name="rows_and_chunks",
    )(where, mine, theirs, cot, cot_far, gain, tokens)


def small_call(kernel, out_shape, *operands, where=None):
    vmem = pl.BlockSpec(memory_space=pltpu.VMEM)
    scalars = () if where is None else (where,)
    return pl.pallas_call(
        kernel,
        out_shape=out_shape,
        in_specs=[pl.BlockSpec(memory_space=pltpu.SMEM)] * len(scalars) + [vmem] * len(operands),
        out_specs=[vmem] * len(out_shape),
        compiler_params=pltpu.CompilerParams(vmem_limit_bytes=8 * 2**20),
        cost_estimate=pl.CostEstimate(flops=0, transcendentals=0, bytes_accessed=0),
    )(*scalars, *operands)


def backs_kernel(rows, weight, *outs):
    count = outs[0].shape[0]
    for k, out in enumerate(outs):
        out[...] = lax.dot_general(
            rows[k * count : (k + 1) * count, :],
            weight[...],
            (((1,), (1,)), ((), ())),
            preferred_element_type=F32,
        ).astype(out.dtype)


def back_sum_kernel(first, *rest):
    terms, (near, far) = rest[:-2], rest[-2:]
    count = near.shape[0]
    for span, out in ((pl.ds(0, count), near), (pl.ds(count, count), far)):
        total = first[span, :]
        for t in terms:
            total = total + t[span, :].astype(F32)
        out[...] = total.astype(out.dtype)


def over_y_kernel(where, own, up, down, got3, got5, kept, *sends):
    count, third = kept.shape[0], len(sends) + 1
    half = own.shape[2]
    for k in range(third):
        place = lax.rem(where[0] + k, third)
        for i in range(count):
            z = i * third + place
            for h in range(2):
                total = own[h, z].astype(F32) + (up[h, z].astype(F32) + down[h, z].astype(F32))
                total = total + (got3[h, z].astype(F32) + got5[h, z].astype(F32))
                out = sends[k - 1] if k else kept
                out[i, h * half : (h + 1) * half] = total.astype(out.dtype)


def over_third_kernel(where, kept, *rest):
    got, (stay, send) = rest[:-2], rest[-2:]
    side = where[1]
    for at, out in ((side, stay), (1 - side, send)):
        total = kept[at]
        for g in got:
            total = total + g[at].astype(F32)
        out[...] = total.astype(out.dtype)


def shift(value, axis, by):
    size = lax.axis_size(axis)
    return lax.ppermute(value, axis, [(i, (i + by) % size) for i in range(size)])


def add(*terms):
    total = terms[0].astype(F32)
    for t in terms[1:]:
        total = total + t.astype(F32)
    return total


def body(normed, weight, cotangent, head_gain):
    nx, ny, nz, nh = (lax.axis_size(a) for a in ("x", "y", "zl", "zh"))
    count, width = normed.shape
    heads = weight.shape[1]
    where = jnp.stack([lax.axis_index(a) for a in ("x", "y")]).astype(jnp.int32)
    zh = lax.axis_index("zh")

    def mirror(value):
        ends = [(i, nz * nh - 1 - i) for i in range(nz * nh)]
        return lax.ppermute(value, ("zl", "zh"), ends)

    peer = mirror(normed)
    own = [normed] + [shift(normed, "x", k) for k in (1, 2, 3)]
    cot = cotangent.reshape(nx, nh, count, heads)
    cot_far = lax.dynamic_index_in_dim(cot, 1 - zh, 1, False)
    cot_far = lax.ppermute(cot_far, "zl", [(i, nz - 1 - i) for i in range(nz)])
    cot = lax.dynamic_index_in_dim(cot, zh, 1, False)
    other = [peer] + [shift(peer, "x", k) for k in (1, 2, 3)]
    other[2], cot_far = lax.optimization_barrier((other[2], cot_far))
    tokens = jnp.concatenate([p for pair in zip(own, other) for p in pair], axis=0)

    mine = jnp.dot(tokens, weight, preferred_element_type=F32)
    theirs = shift(mine, "c", 1)
    factor = 1.0 / math.sqrt(count * nx * nh * ny * nz)
    rows, *c = rows_and_chunks(
        (nx, nh, ny, nz),
        factor,
        where,
        mine,
        theirs,
        cot,
        cot_far,
        head_gain.reshape(1, -1),
        tokens,
    )

    up, down, three, five, own = c
    got_up, got_down = shift(up, "y", 1), shift(down, "y", -1)
    low = jnp.pad(got_up[4:].astype(F32), ((0, 1), (0, 0), (0, 0), (0, 0)))
    high = jnp.pad(got_down[4:].astype(F32), ((1, 0), (0, 0), (0, 0), (0, 0)))
    three = add(three, got_down[2:4], low).astype(BF16)
    five = add(five, got_up[2:4], high).astype(BF16)
    got3, got5 = shift(three, "y", 3), shift(five, "y", -3)

    block = (nh * count, width)
    back = small_call(
        backs_kernel,
        [jax.ShapeDtypeStruct(block, F32)] + [jax.ShapeDtypeStruct(block, BF16)] * (nx - 1),
        rows,
        weight,
    )
    near, far = small_call(
        back_sum_kernel,
        [jax.ShapeDtypeStruct((count, width), t) for t in (F32, BF16)],
        back[0],
        *[shift(back[k], "x", -k) for k in (1, 2, 3)],
    )
    input_grad = add(near, mirror(far)).astype(BF16)

    third = nz // 2
    zl = lax.axis_index("zl")
    spot = jnp.stack([zl % third, zl // third]).astype(jnp.int32)
    blk = 2 * own.shape[2]
    kept, *sends = small_call(
        over_y_kernel,
        [jax.ShapeDtypeStruct((2, blk, heads), t) for t in (F32, *[BF16] * (third - 1))],
        own,
        got_up,
        got_down,
        got3,
        got5,
        where=spot,
    )
    got = []
    for k in range(1, third):
        hop = [(i, i // third * third + (i + k) % third) for i in range(nz)]
        got.append(lax.ppermute(sends[k - 1], "zl", hop))
    stay, send = small_call(
        over_third_kernel,
        [jax.ShapeDtypeStruct((blk, heads), t) for t in (F32, BF16)],
        kept,
        *got,
        where=spot,
    )
    weight_grad = add(stay, shift(send, "zl", third))
    return (input_grad, weight_grad)


def spread(fine):
    return jax.shard_map(
        body,
        mesh=fine,
        in_specs=(
            P(("zl", "y", "x", "zh"), "c"),
            P("c", ("x", "zh")),
            P(("zl", "y"), ("x", "zh")),
            P(),
        ),
        out_specs=(P(("zl", "y", "x", "zh"), "c"), P(("c", "zl", "y"), ("x", "zh"))),
        check_vma=False,
    )


def solution(mesh):
    return spread(Mesh(mesh.devices.reshape(6, 8, 4, 2, 2), ("zl", "y", "x", "zh", "c")))
```
